32 devices in a mesh: section: 4 (over y, x), seq: 8 (over z, core).
Axes of the slice: x: 2, y: 2, z: 4, core: 2. Of those that a mesh axis runs over, the one named last changes fastest.
Arguments:
- features: bfloat16 [4, 1024, 4096], P('section', 'seq'), may hold values from -6 to 6
- queries: bfloat16 [4, 1024, 4096], P('section', 'seq'), may hold values from -52 to 52
- out_grad: bfloat16 [4, 1024, 4096], P('section', 'seq'), may hold values from -0.375 to 0.375
- doc_ids: int32 [4, 1024], P('section', 'seq'), may hold values from 0 to 3, never falling along the last dimension, each value on 1 to 512 neighbouring positions
- key_weight: bfloat16 [4096, 512], P('section'), may hold values from -0.09375 to 0.09375
Outputs:
- value_weight_grad: float32 [4096, 512], P('seq', 'section')
The draws below stay inside these ranges and needn't reach their ends.
All inputs are finite; a program needn't handle non-finite values.
Results may differ from the reference program's by a relative error of at most 0.012.
Values may be sent and summed in bfloat16 or wider, within the bound.
A program may use at most 64 MiB of HBM per device.

```python
import math
import jax
import jax.numpy as jnp
import numpy as np
from jax import lax

D = 4096
HQ = 32
KVH = 4
HD = 128
TOK_DEV = 128
REACH = 4
MOST = 512
LEN = 1024
MB = 4
N_SECTION = 4
N_SEQ = 8


def draw_queries(key, part):
    shape_full = (MB, LEN, HQ * HD)
    values = jnp.clip(jax.random.normal(key, shape_full, jnp.float32), -6.0, 6.0)
    return values.astype(jnp.bfloat16)


def block_levels(key, dims, shards, low, largest):
    def one(position, shards_of):
        heights = jax.random.uniform(jax.random.fold_in(jax.random.fold_in(key, 6), position), (shards_of,), jnp.float32, low / len(shards), largest / len(shards))
        return jnp.repeat(jnp.exp(heights), dims[position] // shards_of).reshape((-1,) + (1,) * (len(dims) - position - 1))

    loudness = one(*shards[0])
    for cut in shards[1:]:
        loudness = loudness * one(*cut)
    return loudness


def split_up(count, total, most, slope):
    loads = [(1 << 20) // math.isqrt(rank ** slope) + 1 for rank in range(2, count + 1)]
    surplus, counts = total - most - (count - 1), [1] * (count - 1)
    while surplus > 0:
        candidates = [i for i in range(count - 1) if counts[i] < most]
        mass, left = sum([loads[i] for i in candidates]), surplus
        for i in candidates:
            addition = min(most - counts[i], max(1, left * loads[i] // mass), surplus)
            counts[i] = counts[i] + addition
            surplus = surplus - addition
    return np.array([most] + counts)


def ragged_sizes(key, amount, total, reach, slope):
    if amount == 2:
        one = jax.random.randint(key, (), max(1, total - reach), min(reach, total - 1) + 1)
        return jnp.stack([one, total - one])
    sizes = jnp.asarray(split_up(amount, total, reach, slope), jnp.int32)
    twos = (amount - 1) // 2
    giver, receiver = sizes[1:1 + 2 * twos:2], sizes[2:2 + 2 * twos:2]
    room = jnp.minimum(giver - 1, reach - receiver)
    moved = jax.random.randint(jax.random.fold_in(key, 1), (twos,), 0, 1 << 20) % (room + 1)
    sizes = sizes.at[1:1 + 2 * twos:2].set(giver - moved).at[2:2 + 2 * twos:2].set(receiver + moved)
    return sizes[jax.random.permutation(jax.random.fold_in(key, 2), amount)]


def centred(stream_key, dims, scale, most, shards=(), kind=jnp.bfloat16):
    loudness = block_levels(stream_key, dims, shards, -0.22, 0.18) if shards else 1.0
    values = jax.random.normal(stream_key, dims, jnp.float32) * scale * loudness
    return jnp.minimum(jnp.maximum(values, -most), most).astype(kind)


def setup_inputs(seed: int = 0) -> dict:
    key_list = jax.random.split(jax.random.key(seed), 6)
    features = centred(key_list[0], (MB, LEN, D), 1.0, 6.0, ((0, 4), (1, 8)))
    queries = draw_queries(jax.random.fold_in(key_list[5], 71), 0)
    out_grad = centred(key_list[2], (MB, LEN, HQ * HD), (4.0 / (TOK_DEV * N_SEQ * N_SECTION) ** 0.5), 0.375, ((0, 4), (1, 8)))
    doc_ids = jax.vmap(lambda own: jnp.searchsorted(jnp.cumsum(ragged_sizes(own, 2 * N_SEQ // REACH, LEN, MOST, 2)), jnp.arange(LEN), side="right"))(jax.random.split(key_list[3], MB)).reshape((MB, LEN)).astype(jnp.int32)
    key_weight = centred(key_list[4], (D, KVH * HD), D ** -0.5, 0.09375, ((0, 4),))
    return {"features": features, "queries": queries, "out_grad": out_grad, "doc_ids": doc_ids, "key_weight": key_weight}


def reference(features, queries, out_grad, doc_ids, key_weight):
    kv_width = KVH * HD
    group_size = HQ // KVH
    margin = REACH * TOK_DEV
    window_len = margin + TOK_DEV
    score_scale = 1.0 / math.sqrt(HD)

    def one_batch(running, items):
        feat_rows, query_all, grad_all, doc_all = items
        keys_all = jnp.dot(feat_rows, key_weight, preferred_element_type=jnp.float32).astype(jnp.bfloat16)
        keys_pad = jnp.concatenate([jnp.zeros((margin, kv_width), keys_all.dtype), keys_all], axis=0)
        docs_pad = jnp.concatenate([jnp.full((margin,), -1, jnp.int32), doc_all.astype(jnp.int32)], axis=0)

        def block(index):
            first_row = (index * TOK_DEV).astype(jnp.int32)
            key_win = lax.dynamic_slice_in_dim(keys_pad, first_row, window_len, 0)
            doc_win = lax.dynamic_slice_in_dim(docs_pad, first_row, window_len, 0)
            query_blk = lax.dynamic_slice_in_dim(query_all, first_row, TOK_DEV, 0)
            grad_blk = lax.dynamic_slice_in_dim(grad_all, first_row, TOK_DEV, 0)
            doc_blk = lax.dynamic_slice_in_dim(doc_all.astype(jnp.int32), first_row, TOK_DEV, 0)
            query_f = query_blk.astype(jnp.float32).reshape(TOK_DEV, KVH, group_size, HD)
            grad_f = grad_blk.astype(jnp.float32).reshape(TOK_DEV, KVH, group_size, HD)
            key_f = key_win.astype(jnp.float32).reshape(window_len, KVH, HD)
            scores = jnp.einsum('tgrd,wgd->tgrw', query_f, key_f) * score_scale
            query_pos = first_row + jnp.arange(TOK_DEV, dtype=jnp.int32)
            key_pos = first_row - margin + jnp.arange(window_len, dtype=jnp.int32)
            visible = (doc_blk[:, None] == doc_win[None, :]) & (key_pos[None, :] <= query_pos[:, None])
            mask_full = visible[:, None, None, :]
            masked = jnp.where(mask_full, scores, -1e+30)
            row_top = lax.optimization_barrier(jnp.max(masked, axis=3, keepdims=True))
            weights_exp = jnp.where(mask_full, jnp.exp(masked - row_top), 0.0)
            prob_rows = (weights_exp / lax.optimization_barrier(jnp.sum(weights_exp, axis=3, keepdims=True))).astype(jnp.bfloat16)
            window_grad = jnp.einsum('tgrw,tgrd->wgd', prob_rows.astype(jnp.float32), grad_f)
            return window_grad.reshape(REACH + 1, TOK_DEV, kv_width)
        pieces = lax.map(block, jnp.arange(N_SEQ, dtype=jnp.int32))
        padded = jnp.concatenate([pieces, jnp.zeros((REACH, REACH + 1, TOK_DEV, kv_width), pieces.dtype)], axis=0)
        summed = jnp.zeros((N_SEQ, TOK_DEV, kv_width), pieces.dtype)
        for hop_count in range(REACH + 1):
            summed = summed + padded[hop_count:hop_count + N_SEQ, REACH - hop_count]
        value_grad = summed.reshape(N_SEQ * TOK_DEV, kv_width).astype(jnp.bfloat16)
        contrib = jnp.dot(feat_rows.T, value_grad, preferred_element_type=jnp.float32)
        return (running + contrib, None)
    start_value = jnp.zeros((D, kv_width), jnp.float32)
    result, unused = lax.scan(one_batch, start_value, (features, queries, out_grad, doc_ids))
    return result
```

```python
import functools
import math

import jax
import jax.numpy as jnp
from jax import lax
from jax.experimental import pallas as pl
from jax.experimental.pallas import tpu as pltpu
from jax.sharding import PartitionSpec as P

HQ = 32
KVH = 4
HD = 128
MOST = 512
GROUP = HQ // KVH
PAIR = 2
MESH = pl.DeviceIdType.MESH
F32 = jnp.float32
BF16 = jnp.bfloat16


def flip(index, bits):
    bit = 1
    while bit <= bits:
        if bits & bit:
            index = index + bit * (1 - 2 * lax.rem(lax.div(index, bit), 2))
        bit *= 2
    return index


def kernel(
    n_sec, n_seq, reach,
    tok_hbm, qry_hbm, grd_hbm, doc_ref, kw_hbm,
    out_ref,
    tok, qry, grd, w_buf, f_buf, f_t, keys, docs, bias, ret_send, ret_recv, own, vg,
    rs_send, rs_recv,
    local_sem, w_ssem, w_rsem, x_ssem, x_rsem, f_ssem, f_rsem, d_ssem, d_rsem,
    k_ssem, k_rsem, r_ssem, r_rsem, v_ssem, v_rsem, s_ssem, s_rsem,
):
    sec, seq = lax.axis_index("section"), lax.axis_index("seq")
    core = lax.rem(seq, 2)
    n_tok = tok.shape[0]
    half = w_buf.shape[2]
    shard = 2 * half
    f_cols = f_buf.shape[2]
    per_head = n_sec // KVH
    cs = rs_send.shape[2]

    def remote(src, dst, ssem, rsem, to_sec, to_seq):
        return pltpu.make_async_remote_copy(
            src_ref=src, dst_ref=dst, send_sem=ssem, recv_sem=rsem,
            device_id=(to_sec, to_seq), device_id_type=MESH,
        )

    loc_w = pltpu.make_async_copy(kw_hbm, w_buf.at[0], local_sem.at[0])
    loc_t = pltpu.make_async_copy(tok_hbm, tok, local_sem.at[1])
    loc_q = pltpu.make_async_copy(qry_hbm, qry, local_sem.at[2])
    loc_g = pltpu.make_async_copy(grd_hbm, grd, local_sem.at[3])

    barrier = pltpu.get_barrier_semaphore()
    for d in range(1, n_sec):
        pl.semaphore_signal(barrier, inc=1, device_id=(flip(sec, d), seq), device_id_type=MESH)
    for d in range(1, n_seq):
        pl.semaphore_signal(barrier, inc=1, device_id=(sec, flip(seq, d)), device_id_type=MESH)
    loc_w.start()
    loc_t.start()
    loc_q.start()
    loc_g.start()
    pl.semaphore_wait(barrier, n_sec + n_seq - 2)

    sends = []

    def launch(copy):
        copy.start()
        sends.append((None, copy))

    w_in = [None] + [
        remote(kw_hbm.at[core], w_buf.at[d, core], w_ssem.at[d - 1], w_rsem.at[d - 1], flip(sec, d), seq)
        for d in range(1, n_sec)
    ]
    for d in range(1, n_sec):
        launch(w_in[d])

    def hop(h, src, dst, ssem, rsem, by):
        copy = remote(src, dst, ssem, rsem, sec, seq + by)
        return copy

    docs[0] = doc_ref[...]
    d_out = []
    for h in range(1, reach + 1):
        copy = remote(doc_ref, docs.at[h], d_ssem.at[h - 1], d_rsem.at[h - 1], sec, seq + h)
        d_out.append(copy)
        has_later = seq + h < n_seq
        pl.when(has_later)(copy.start)
        sends.append((has_later, copy))

    f_in = [None]
    for d in range(1, n_seq):
        peer = flip(seq, d)
        cols = pl.ds(pl.multiple_of(peer * f_cols, f_cols), f_cols)
        copy = remote(tok_hbm.at[:, cols], f_buf.at[d], f_ssem.at[d - 1], f_rsem.at[d - 1], sec, peer)
        launch(copy)
        f_in.append(copy)

    for h in range(1, reach + 1):
        @pl.when(seq < h)
        def _(h=h):
            docs[h] = jnp.full(docs.shape[1:], -1, jnp.int32)
            keys[h] = jnp.zeros(keys.shape[1:], BF16)

        @pl.when(seq + h >= n_seq)
        def _(h=h):
            for k in range(KVH):
                ret_recv[k, h - 1] = jnp.zeros(ret_recv.shape[2:], BF16)

    loc_t.wait()
    loc_w.wait()

    def project(d, which):
        row = pl.multiple_of(flip(sec, d) * shard + which * half, half)
        return jnp.dot(tok[:, pl.ds(row, half)], w_buf[d, which], preferred_element_type=F32)

    total = project(0, 0) + project(0, 1)

    own_row = docs[0]
    query_doc = own_row.astype(F32)
    key_at = lax.broadcasted_iota(jnp.int32, (n_tok, n_tok), 0)
    query_at = lax.broadcasted_iota(jnp.int32, (n_tok, n_tok), 1)
    for h in range(reach + 1):
        if h:
            pl.when(seq >= h)(d_out[h - 1].wait_recv)
        key_doc = jnp.broadcast_to(docs[h].astype(F32), (n_tok, n_tok)).T
        seen = key_doc == jnp.broadcast_to(query_doc, (n_tok, n_tok))
        if h == 0:
            seen = seen & (key_at <= query_at)
        bias[pl.ds(h * n_tok, n_tok), :] = jnp.where(seen, 0.0, -1e30)

    x_in = [None]
    for d in range(1, n_sec):
        w_in[d].wait_recv()
        copy = remote(
            w_buf.at[d, core], w_buf.at[d, core], x_ssem.at[d - 1], x_rsem.at[d - 1], sec, flip(seq, 1)
        )
        launch(copy)
        x_in.append(remote(
            w_buf.at[d, 1 - core], w_buf.at[d, 1 - core], x_ssem.at[d - 1], x_rsem.at[d - 1],
            sec, flip(seq, 1),
        ))
        total = total + project(d, core)
    for d in range(1, n_sec):
        x_in[d].wait_recv()
        total = total + project(d, 1 - core)
    keys[0] = total.astype(BF16)

    k_in = []
    for h in range(1, reach + 1):
        copy = remote(keys.at[0], keys.at[h], k_ssem.at[h - 1], k_rsem.at[h - 1], sec, seq + h)
        has_later = seq + h < n_seq
        pl.when(has_later)(copy.start)
        sends.append((has_later, copy))
        k_in.append(copy)

    own_cols = pl.ds(pl.multiple_of(seq * f_cols, f_cols), f_cols)
    f_t[:, 0:n_tok] = tok[:, own_cols].T
    for d in range(1, n_seq):
        f_in[d].wait_recv()
        f_t[:, d * n_tok : (d + 1) * n_tok] = f_buf[d].T

    loc_q.wait()
    loc_g.wait()
    for h in range(1, reach + 1):
        pl.when(seq >= h)(k_in[h - 1].wait_recv)

    scale = math.log2(math.e) / math.sqrt(HD)
    window = (reach + 1) * n_tok

    def head_of(k):
        return lax.rem(lax.div(sec, per_head) + 1 + k, KVH)

    r_in = {}

    def attend(k):
        head = head_of(k)
        key_head = keys[:, :, pl.ds(pl.multiple_of(head * HD, HD), HD)].reshape(window, HD)
        mask = jnp.concatenate([bias[...]] * PAIR, axis=1)
        acc = jnp.zeros((window, HD), F32)
        for r in range(0, GROUP, PAIR):
            def rows(ref):
                base = head * (GROUP * HD)
                parts = [
                    ref[:, pl.ds(pl.multiple_of(base + (r + i) * HD, HD), HD)] for i in range(PAIR)
                ]
                return jnp.concatenate(parts, axis=0)

            scores = lax.dot_general(
                key_head, rows(qry), (((1,), (1,)), ((), ())), preferred_element_type=F32
            ) * scale + mask
            top = jnp.max(scores, axis=0, keepdims=True)
            e = jnp.exp2(scores - top)
            p = e * (1.0 / jnp.sum(e, axis=0, keepdims=True))
            acc = acc + jnp.dot(p.astype(BF16), rows(grd), preferred_element_type=F32)
        own[k] = acc[0:n_tok]
        for h in range(1, reach + 1):
            ret_send[k, h - 1] = acc[h * n_tok : (h + 1) * n_tok].astype(BF16)
            copy = remote(
                ret_send.at[k, h - 1], ret_recv.at[k, h - 1],
                r_ssem.at[k, h - 1], r_rsem.at[k, h - 1], sec, seq - h,
            )
            pl.when(seq >= h)(copy.start)
            sends.append((seq >= h, copy))
            r_in[k, h] = copy

    v_in = {}

    def combine(k):
        value = own[k]
        for h in range(1, reach + 1):
            pl.when(seq + h < n_seq)(r_in[k, h].wait_recv)
            value = value + ret_recv[k, h - 1].astype(F32)
        vg[k, 0] = value.astype(BF16)
        for d in range(1, n_seq):
            copy = remote(
                vg.at[k, 0], vg.at[k, d], v_ssem.at[k, d - 1], v_rsem.at[k, d - 1], sec, flip(seq, d)
            )
            launch(copy)
            v_in[k, d] = copy

    def finish(k):
        for d in range(1, n_seq):
            v_in[k, d].wait_recv()
        result = jnp.dot(
            f_t[...], vg[k].reshape(n_seq * n_tok, HD), preferred_element_type=F32
        )
        head = head_of(k)
        for i in range(per_head):
            piece = result[:, i * cs : (i + 1) * cs]
            slot = k * per_head + i
            to = head * per_head + i

            def give(slot=slot, to=to, piece=piece):
                rs_send[slot] = piece.astype(BF16)
                remote(
                    rs_send.at[slot], rs_recv.at[sec], s_ssem.at[slot], s_rsem.at[sec], to, seq
                ).start()

            copy = remote(
                rs_send.at[slot], rs_recv.at[sec], s_ssem.at[slot], s_rsem.at[sec], to, seq
            )
            if k < KVH - 1:
                give()
                sends.append((None, copy))
            else:
                if per_head > 1:
                    pl.when(to != sec)(give)
                    sends.append((to != sec, copy))

                @pl.when(to == sec)
                def _(piece=piece):
                    out_ref[...] = piece

    for step in range(KVH + 2):
        if step < KVH:
            attend(step)
        if 0 <= step - 1 < KVH:
            combine(step - 1)
        if 0 <= step - 2 < KVH:
            finish(step - 2)

    final = out_ref[...]
    for d in range(1, n_sec):
        src = flip(sec, d)
        remote(rs_recv.at[src], rs_recv.at[src], s_ssem.at[0], s_rsem.at[src], src, seq).wait_recv()
        final = final + rs_recv[src].astype(F32)
    out_ref[...] = final

    for condition, copy in sends:
        if condition is None:
            copy.wait_send()
        else:
            pl.when(condition)(copy.wait_send)


def on_device(n_sec, n_seq, features, queries, out_grad, doc_ids, key_weight):
    tokens = features[0]
    n_tok, width = tokens.shape
    rows, kv_width = key_weight.shape
    reach = min(n_seq - 1, -(-(MOST - 1) // n_tok))
    half = rows // 2
    f_cols = width // n_seq
    cs = kv_width // n_sec
    dma = lambda *shape: pltpu.SemaphoreType.DMA(shape)
    any_spec = pl.BlockSpec(memory_space=pl.ANY)
    vmem_spec = pl.BlockSpec(memory_space=pltpu.VMEM)
    return pl.pallas_call(
        functools.partial(kernel, n_sec, n_seq, reach),
        out_shape=jax.ShapeDtypeStruct((f_cols, cs), F32),
        in_specs=[any_spec, any_spec, any_spec, vmem_spec, any_spec],
        out_specs=vmem_spec,
        scratch_shapes=[
            pltpu.VMEM((n_tok, width), BF16),
            pltpu.VMEM((n_tok, HQ * HD), BF16),
            pltpu.VMEM((n_tok, HQ * HD), BF16),
            pltpu.VMEM((n_sec, 2, half, kv_width), BF16),
            pltpu.VMEM((n_seq, n_tok, f_cols), BF16),
            pltpu.VMEM((f_cols, n_seq * n_tok), BF16),
            pltpu.VMEM((reach + 1, n_tok, kv_width), BF16),
            pltpu.VMEM((reach + 1, 1, n_tok), jnp.int32),
            pltpu.VMEM(((reach + 1) * n_tok, n_tok), F32),
            pltpu.VMEM((KVH, reach, n_tok, HD), BF16),
            pltpu.VMEM((KVH, reach, n_tok, HD), BF16),
            pltpu.VMEM((KVH, n_tok, HD), F32),
            pltpu.VMEM((KVH, n_seq, n_tok, HD), BF16),
            pltpu.VMEM((n_sec, f_cols, cs), BF16),
            pltpu.VMEM((n_sec, f_cols, cs), BF16),
            dma(4),
            dma(n_sec - 1), dma(n_sec - 1),
            dma(n_sec - 1), dma(n_sec - 1),
            dma(n_seq - 1), dma(n_seq - 1),
            dma(reach), dma(reach),
            dma(reach), dma(reach),
            dma(KVH, reach), dma(KVH, reach),
            dma(KVH, n_seq - 1), dma(KVH, n_seq - 1),
            dma(n_sec), dma(n_sec),
        ],
        compiler_params=pltpu.CompilerParams(
            collective_id=0, has_side_effects=True, vmem_limit_bytes=48 * 1024 * 1024
        ),
    )(tokens, queries[0], out_grad[0], doc_ids, key_weight.reshape(2, half, kv_width))


def solution(mesh):
    n_sec, n_seq = mesh.shape["section"], mesh.shape["seq"]
    return jax.shard_map(
        functools.partial(on_device, n_sec, n_seq),
        mesh=mesh,
        in_specs=(
            P("section", "seq", None),
            P("section", "seq", None),
            P("section", "seq", None),
            P("section", "seq"),
            P("section", None),
        ),
        out_specs=P("seq", "section"),
        check_vma=False,
    )
```

```python
import functools
import math

import jax
import jax.numpy as jnp
from jax import lax
from jax.experimental import pallas as pl
from jax.experimental.pallas import tpu as pltpu
from jax.sharding import PartitionSpec as P

HQ = 32
KVH = 4
HD = 128
MOST = 512
GROUP = HQ // KVH
PAIR = 2
MESH = pl.DeviceIdType.MESH
F32 = jnp.float32
BF16 = jnp.bfloat16


def flip(index, bits):
    bit = 1
    while bit <= bits:
        if bits & bit:
            index = index + bit * (1 - 2 * lax.rem(lax.div(index, bit), 2))
        bit *= 2
    return index


def kernel(
    n_sec, n_seq, reach,
    tok_hbm, qry_hbm, grd_hbm, doc_ref, kw_hbm,
    out_ref,
    tok, qry, grd, w_buf, f_buf, f_t, keys, docs, bias, ret_send, ret_recv, own, vg,
    rs_send, rs_recv, ex_send, ex_recv, total_ref,
    local_sem, w_ssem, w_rsem, x_ssem, x_rsem, f_ssem, f_rsem, d_ssem, d_rsem,
    k_ssem, k_rsem, r_ssem, r_rsem, v_ssem, v_rsem, s_ssem, s_rsem, e_ssem, e_rsem,
):
    sec, seq = lax.axis_index("section"), lax.axis_index("seq")
    core = lax.rem(seq, 2)
    n_tok = tok.shape[0]
    half = w_buf.shape[2]
    shard = 2 * half
    f_cols = f_buf.shape[3]
    group = n_seq // 2
    other = flip(seq, group)
    per_head = n_sec // KVH
    cs = rs_send.shape[2]

    def remote(src, dst, ssem, rsem, to_sec, to_seq):
        return pltpu.make_async_remote_copy(
            src_ref=src, dst_ref=dst, send_sem=ssem, recv_sem=rsem,
            device_id=(to_sec, to_seq), device_id_type=MESH,
        )

    loc_w = pltpu.make_async_copy(kw_hbm, w_buf.at[0], local_sem.at[0])
    loc_t = pltpu.make_async_copy(tok_hbm, tok, local_sem.at[1])
    loc_q = pltpu.make_async_copy(qry_hbm, qry, local_sem.at[2])
    loc_g = pltpu.make_async_copy(grd_hbm, grd, local_sem.at[3])

    barrier = pltpu.get_barrier_semaphore()
    for d in range(1, n_sec):
        pl.semaphore_signal(barrier, inc=1, device_id=(flip(sec, d), seq), device_id_type=MESH)
    for d in range(1, n_seq):
        pl.semaphore_signal(barrier, inc=1, device_id=(sec, flip(seq, d)), device_id_type=MESH)
    loc_w.start()
    loc_t.start()
    loc_q.start()
    loc_g.start()
    pl.semaphore_wait(barrier, n_sec + n_seq - 2)

    sends = []

    def launch(copy):
        copy.start()
        sends.append((None, copy))

    w_in = [None] + [
        remote(kw_hbm.at[core], w_buf.at[d, core], w_ssem.at[d - 1], w_rsem.at[d - 1], flip(sec, d), seq)
        for d in range(1, n_sec)
    ]
    for d in range(1, n_sec):
        launch(w_in[d])

    docs[0] = doc_ref[...]
    d_out = []
    for h in range(1, reach + 1):
        copy = remote(doc_ref, docs.at[h], d_ssem.at[h - 1], d_rsem.at[h - 1], sec, seq + h)
        d_out.append(copy)
        has_later = seq + h < n_seq
        pl.when(has_later)(copy.start)
        sends.append((has_later, copy))

    def columns_of(place):
        return pl.ds(pl.multiple_of(place * f_cols, f_cols), f_cols)

    f_in = {}
    for d in range(1, group):
        peer = flip(seq, d)
        for c in range(2):
            copy = remote(
                tok_hbm.at[:, columns_of(flip(peer, c * group))], f_buf.at[d, c],
                f_ssem.at[d - 1, c], f_rsem.at[d - 1, c], sec, peer,
            )
            launch(copy)
            f_in[d, c] = copy

    for h in range(1, reach + 1):
        @pl.when(seq < h)
        def _(h=h):
            docs[h] = jnp.full(docs.shape[1:], -1, jnp.int32)
            keys[h] = jnp.zeros(keys.shape[1:], BF16)

        @pl.when(seq + h >= n_seq)
        def _(h=h):
            for k in range(KVH):
                ret_recv[k, h - 1] = jnp.zeros(ret_recv.shape[2:], BF16)

    loc_t.wait()
    loc_w.wait()

    def project(d, which):
        row = pl.multiple_of(flip(sec, d) * shard + which * half, half)
        return jnp.dot(tok[:, pl.ds(row, half)], w_buf[d, which], preferred_element_type=F32)

    total = project(0, 0) + project(0, 1)

    own_row = docs[0]
    query_doc = own_row.astype(F32)
    key_at = lax.broadcasted_iota(jnp.int32, (n_tok, n_tok), 0)
    query_at = lax.broadcasted_iota(jnp.int32, (n_tok, n_tok), 1)
    for h in range(reach + 1):
        if h:
            pl.when(seq >= h)(d_out[h - 1].wait_recv)
        key_doc = jnp.broadcast_to(docs[h].astype(F32), (n_tok, n_tok)).T
        seen = key_doc == jnp.broadcast_to(query_doc, (n_tok, n_tok))
        if h == 0:
            seen = seen & (key_at <= query_at)
        bias[pl.ds(h * n_tok, n_tok), :] = jnp.where(seen, 0.0, -1e30)

    x_in = [None]
    for d in range(1, n_sec):
        w_in[d].wait_recv()
        copy = remote(
            w_buf.at[d, core], w_buf.at[d, core], x_ssem.at[d - 1], x_rsem.at[d - 1], sec, flip(seq, 1)
        )
        launch(copy)
        x_in.append(remote(
            w_buf.at[d, 1 - core], w_buf.at[d, 1 - core], x_ssem.at[d - 1], x_rsem.at[d - 1],
            sec, flip(seq, 1),
        ))
        total = total + project(d, core)
    for d in range(1, n_sec):
        x_in[d].wait_recv()
        total = total + project(d, 1 - core)
    keys[0] = total.astype(BF16)

    k_in = []
    for h in range(1, reach + 1):
        copy = remote(keys.at[0], keys.at[h], k_ssem.at[h - 1], k_rsem.at[h - 1], sec, seq + h)
        has_later = seq + h < n_seq
        pl.when(has_later)(copy.start)
        sends.append((has_later, copy))
        k_in.append(copy)

    for c in range(2):
        rows_c = pl.ds(c * f_cols, f_cols)
        f_t[rows_c, 0:n_tok] = tok[:, columns_of(flip(seq, c * group))].T
        for d in range(1, group):
            f_in[d, c].wait_recv()
            f_t[rows_c, d * n_tok : (d + 1) * n_tok] = f_buf[d, c].T

    loc_q.wait()
    loc_g.wait()
    for h in range(1, reach + 1):
        pl.when(seq >= h)(k_in[h - 1].wait_recv)

    scale = math.log2(math.e) / math.sqrt(HD)
    window = (reach + 1) * n_tok

    def head_of(k):
        return lax.rem(lax.div(sec, per_head) + 1 + k, KVH)

    r_in = {}

    def attend(k):
        head = head_of(k)
        key_head = keys[:, :, pl.ds(pl.multiple_of(head * HD, HD), HD)].reshape(window, HD)
        mask = jnp.concatenate([bias[...]] * PAIR, axis=1)
        acc = jnp.zeros((window, HD), F32)
        for r in range(0, GROUP, PAIR):
            def rows(ref):
                base = head * (GROUP * HD)
                parts = [
                    ref[:, pl.ds(pl.multiple_of(base + (r + i) * HD, HD), HD)] for i in range(PAIR)
                ]
                return jnp.concatenate(parts, axis=0)

            scores = lax.dot_general(
                key_head, rows(qry), (((1,), (1,)), ((), ())), preferred_element_type=F32
            ) * scale + mask
            top = jnp.max(scores, axis=0, keepdims=True)
            e = jnp.exp2(scores - top)
            p = e * (1.0 / jnp.sum(e, axis=0, keepdims=True))
            acc = acc + jnp.dot(p.astype(BF16), rows(grd), preferred_element_type=F32)
        own[k] = acc[0:n_tok]
        for h in range(1, reach + 1):
            ret_send[k, h - 1] = acc[h * n_tok : (h + 1) * n_tok].astype(BF16)
            copy = remote(
                ret_send.at[k, h - 1], ret_recv.at[k, h - 1],
                r_ssem.at[k, h - 1], r_rsem.at[k, h - 1], sec, seq - h,
            )
            pl.when(seq >= h)(copy.start)
            sends.append((seq >= h, copy))
            r_in[k, h] = copy

    v_in = {}

    def combine(k):
        value = own[k]
        for h in range(1, reach + 1):
            pl.when(seq + h < n_seq)(r_in[k, h].wait_recv)
            value = value + ret_recv[k, h - 1].astype(F32)
        vg[k, 0] = value.astype(BF16)
        for d in range(1, group):
            copy = remote(
                vg.at[k, 0], vg.at[k, d], v_ssem.at[k, d - 1], v_rsem.at[k, d - 1], sec, flip(seq, d)
            )
            launch(copy)
            v_in[k, d] = copy

    def finish(k):
        for d in range(1, group):
            v_in[k, d].wait_recv()
        result = jnp.dot(
            f_t[...], vg[k].reshape(group * n_tok, HD), preferred_element_type=F32
        )
        head = head_of(k)
        for i in range(per_head):
            piece = result[:, i * cs : (i + 1) * cs]
            slot = k * per_head + i
            to = head * per_head + i

            def give(slot=slot, to=to, piece=piece):
                rs_send[slot] = piece.astype(BF16)
                remote(
                    rs_send.at[slot], rs_recv.at[sec], s_ssem.at[slot], s_rsem.at[sec], to, seq
                ).start()

            copy = remote(
                rs_send.at[slot], rs_recv.at[sec], s_ssem.at[slot], s_rsem.at[sec], to, seq
            )
            if k < KVH - 1:
                give()
                sends.append((None, copy))
            else:
                if per_head > 1:
                    pl.when(to != sec)(give)
                    sends.append((to != sec, copy))

                @pl.when(to == sec)
                def _(piece=piece):
                    total_ref[...] = piece

    for step in range(KVH + 2):
        if step < KVH:
            attend(step)
        if 0 <= step - 1 < KVH:
            combine(step - 1)
        if 0 <= step - 2 < KVH:
            finish(step - 2)

    sources = [flip(sec, d) for d in range(1, n_sec)]
    for src in sources:
        remote(rs_recv.at[src], rs_recv.at[src], s_ssem.at[0], s_rsem.at[src], src, seq).wait_recv()
    theirs = pl.ds(f_cols, f_cols)
    away = total_ref[theirs, :]
    for src in sources:
        away = away + rs_recv[src, theirs, :].astype(F32)
    ex_send[...] = away.astype(BF16)
    swap = remote(ex_send, ex_recv, e_ssem.at[0], e_rsem.at[0], sec, other)
    launch(swap)
    mine = pl.ds(0, f_cols)
    final = total_ref[mine, :]
    for src in sources:
        final = final + rs_recv[src, mine, :].astype(F32)
    swap.wait_recv()
    out_ref[...] = final + ex_recv[...].astype(F32)

    for condition, copy in sends:
        if condition is None:
            copy.wait_send()
        else:
            pl.when(condition)(copy.wait_send)


def on_device(n_sec, n_seq, features, queries, out_grad, doc_ids, key_weight):
    tokens = features[0]
    n_tok, width = tokens.shape
    rows, kv_width = key_weight.shape
    reach = min(n_seq - 1, -(-(MOST - 1) // n_tok))
    half = rows // 2
    f_cols = width // n_seq
    group = n_seq // 2
    cs = kv_width // n_sec
    dma = lambda *shape: pltpu.SemaphoreType.DMA(shape)
    any_spec = pl.BlockSpec(memory_space=pltpu.HBM)
    vmem_spec = pl.BlockSpec(memory_space=pltpu.VMEM)
    return pl.pallas_call(
        functools.partial(kernel, n_sec, n_seq, reach),
        out_shape=jax.ShapeDtypeStruct((f_cols, cs), F32),
        in_specs=[any_spec, any_spec, any_spec, vmem_spec, any_spec],
        out_specs=vmem_spec,
        scratch_shapes=[
            pltpu.VMEM((n_tok, width), BF16),
            pltpu.VMEM((n_tok, HQ * HD), BF16),
            pltpu.VMEM((n_tok, HQ * HD), BF16),
            pltpu.VMEM((n_sec, 2, half, kv_width), BF16),
            pltpu.VMEM((group, 2, n_tok, f_cols), BF16),
            pltpu.VMEM((2 * f_cols, group * n_tok), BF16),
            pltpu.VMEM((reach + 1, n_tok, kv_width), BF16),
            pltpu.VMEM((reach + 1, 1, n_tok), jnp.int32),
            pltpu.VMEM(((reach + 1) * n_tok, n_tok), F32),
            pltpu.VMEM((KVH, reach, n_tok, HD), BF16),
            pltpu.VMEM((KVH, reach, n_tok, HD), BF16),
            pltpu.VMEM((KVH, n_tok, HD), F32),
            pltpu.VMEM((KVH, group, n_tok, HD), BF16),
            pltpu.VMEM((n_sec, 2 * f_cols, cs), BF16),
            pltpu.VMEM((n_sec, 2 * f_cols, cs), BF16),
            pltpu.VMEM((f_cols, cs), BF16),
            pltpu.VMEM((f_cols, cs), BF16),
            pltpu.VMEM((2 * f_cols, cs), F32),
            dma(4),
            dma(n_sec - 1), dma(n_sec - 1),
            dma(n_sec - 1), dma(n_sec - 1),
            dma(group - 1, 2), dma(group - 1, 2),
            dma(reach), dma(reach),
            dma(reach), dma(reach),
            dma(KVH, reach), dma(KVH, reach),
            dma(KVH, group - 1), dma(KVH, group - 1),
            dma(n_sec), dma(n_sec),
            dma(1), dma(1),
        ],
        compiler_params=pltpu.CompilerParams(
            collective_id=0, has_side_effects=True, vmem_limit_bytes=60 * 1024 * 1024
        ),
    )(tokens, queries[0], out_grad[0], doc_ids, key_weight.reshape(2, half, kv_width))


def solution(mesh):
    n_sec, n_seq = mesh.shape["section"], mesh.shape["seq"]
    return jax.shard_map(
        functools.partial(on_device, n_sec, n_seq),
        mesh=mesh,
        in_specs=(
            P("section", "seq", None),
            P("section", "seq", None),
            P("section", "seq", None),
            P("section", "seq"),
            P("section", None),
        ),
        out_specs=P("seq", "section"),
        check_vma=False,
    )
```

```python
import functools
import math

import jax
import jax.numpy as jnp
from jax import lax
from jax.experimental import pallas as pl
from jax.experimental.pallas import tpu as pltpu
from jax.sharding import PartitionSpec as P

HQ = 32
KVH = 4
HD = 128
MOST = 512
GROUP = HQ // KVH
PAIR = 2
MESH = pl.DeviceIdType.MESH
F32 = jnp.float32
BF16 = jnp.bfloat16


def flip(index, bits):
    bit = 1
    while bit <= bits:
        if bits & bit:
            index = index + bit * (1 - 2 * lax.rem(lax.div(index, bit), 2))
        bit *= 2
    return index


def kernel(
    n_sec, n_seq, reach,
    tok_hbm, qry_hbm, grd_hbm, doc_ref, kw_hbm,
    out_ref,
    tok, qry, grd, w_buf, f_buf, f_t, keys, docs, bias, ret_send, ret_recv, own, vg,
    rs_send, rs_recv, ex_send, ex_recv, total_ref,
    local_sem, w_ssem, w_rsem, x_ssem, x_rsem, f_ssem, f_rsem, d_ssem, d_rsem,
    k_ssem, k_rsem, r_ssem, r_rsem, v_ssem, v_rsem, s_ssem, s_rsem, e_ssem, e_rsem,
):
    sec, seq = lax.axis_index("section"), lax.axis_index("seq")
    core = lax.rem(seq, 2)
    n_tok = tok.shape[0]
    half = w_buf.shape[2]
    shard = 2 * half
    f_cols = f_buf.shape[3]
    group = n_seq // 2
    other = flip(seq, group)
    per_head = n_sec // KVH
    cs = rs_send.shape[2]

    def remote(src, dst, ssem, rsem, to_sec, to_seq):
        return pltpu.make_async_remote_copy(
            src_ref=src, dst_ref=dst, send_sem=ssem, recv_sem=rsem,
            device_id=(to_sec, to_seq), device_id_type=MESH,
        )

    loc_w = pltpu.make_async_copy(kw_hbm, w_buf.at[0], local_sem.at[0])
    loc_t = pltpu.make_async_copy(tok_hbm, tok, local_sem.at[1])
    loc_q = pltpu.make_async_copy(qry_hbm, qry, local_sem.at[2])
    loc_g = pltpu.make_async_copy(grd_hbm, grd, local_sem.at[3])

    barrier = pltpu.get_barrier_semaphore()
    for d in range(1, n_sec):
        pl.semaphore_signal(barrier, inc=1, device_id=(flip(sec, d), seq), device_id_type=MESH)
    for d in range(1, n_seq):
        pl.semaphore_signal(barrier, inc=1, device_id=(sec, flip(seq, d)), device_id_type=MESH)
    loc_w.start()
    loc_t.start()
    loc_q.start()
    loc_g.start()
    pl.semaphore_wait(barrier, n_sec + n_seq - 2)

    sends = []

    def launch(copy):
        copy.start()
        sends.append((None, copy))

    w_in = [None] + [
        remote(kw_hbm.at[core], w_buf.at[d, core], w_ssem.at[d - 1], w_rsem.at[d - 1], flip(sec, d), seq)
        for d in range(1, n_sec)
    ]
    relayed = n_sec == 4
    for d in range(1, n_sec - 1 if relayed else n_sec):
        launch(w_in[d])
    part = half // 2
    relay = [
        remote(
            w_buf.at[d, core, pl.ds(i * part, part)], w_buf.at[3, core, pl.ds(i * part, part)],
            w_ssem.at[2 + i], w_rsem.at[2 + i], flip(sec, 3 - d), seq,
        )
        for i, d in enumerate((1, 2))
    ] if relayed else []

    docs[0] = doc_ref[...]
    d_out = []
    for h in range(1, reach + 1):
        copy = remote(doc_ref, docs.at[h], d_ssem.at[h - 1], d_rsem.at[h - 1], sec, seq + h)
        d_out.append(copy)
        has_later = seq + h < n_seq
        pl.when(has_later)(copy.start)
        sends.append((has_later, copy))

    def columns_of(place):
        return pl.ds(pl.multiple_of(place * f_cols, f_cols), f_cols)

    f_in = {}
    for d in range(1, group):
        peer = flip(seq, d)
        for c in range(2):
            copy = remote(
                tok_hbm.at[:, columns_of(flip(peer, c * group))], f_buf.at[d, c],
                f_ssem.at[d - 1, c], f_rsem.at[d - 1, c], sec, peer,
            )
            launch(copy)
            f_in[d, c] = copy

    for h in range(1, reach + 1):
        @pl.when(seq < h)
        def _(h=h):
            docs[h] = jnp.full(docs.shape[1:], -1, jnp.int32)
            keys[h] = jnp.zeros(keys.shape[1:], BF16)

        @pl.when(seq + h >= n_seq)
        def _(h=h):
            for k in range(KVH):
                ret_recv[k, h - 1] = jnp.zeros(ret_recv.shape[2:], BF16)

    loc_t.wait()
    loc_w.wait()

    def project(d, which):
        row = pl.multiple_of(flip(sec, d) * shard + which * half, half)
        return jnp.dot(tok[:, pl.ds(row, half)], w_buf[d, which], preferred_element_type=F32)

    total = project(0, 0) + project(0, 1)

    own_row = docs[0]
    query_doc = own_row.astype(F32)
    key_at = lax.broadcasted_iota(jnp.int32, (n_tok, n_tok), 0)
    query_at = lax.broadcasted_iota(jnp.int32, (n_tok, n_tok), 1)
    for h in range(reach + 1):
        if h:
            pl.when(seq >= h)(d_out[h - 1].wait_recv)
        key_doc = jnp.broadcast_to(docs[h].astype(F32), (n_tok, n_tok)).T
        seen = key_doc == jnp.broadcast_to(query_doc, (n_tok, n_tok))
        if h == 0:
            seen = seen & (key_at <= query_at)
        bias[pl.ds(h * n_tok, n_tok), :] = jnp.where(seen, 0.0, -1e30)

    x_in = [None]
    for d in range(1, n_sec):
        if relayed and d == 3:
            for copy in relay:
                copy.wait_recv()
        else:
            w_in[d].wait_recv()
            if relayed:
                launch(relay[d - 1])
        copy = remote(
            w_buf.at[d, core], w_buf.at[d, core], x_ssem.at[d - 1], x_rsem.at[d - 1], sec, flip(seq, 1)
        )
        launch(copy)
        x_in.append(remote(
            w_buf.at[d, 1 - core], w_buf.at[d, 1 - core], x_ssem.at[d - 1], x_rsem.at[d - 1],
            sec, flip(seq, 1),
        ))
        total = total + project(d, core)
    for d in range(1, n_sec):
        x_in[d].wait_recv()
        total = total + project(d, 1 - core)
    keys[0] = total.astype(BF16)

    k_in = []
    for h in range(1, reach + 1):
        copy = remote(keys.at[0], keys.at[h], k_ssem.at[h - 1], k_rsem.at[h - 1], sec, seq + h)
        has_later = seq + h < n_seq
        pl.when(has_later)(copy.start)
        sends.append((has_later, copy))
        k_in.append(copy)

    for c in range(2):
        rows_c = pl.ds(c * f_cols, f_cols)
        f_t[rows_c, 0:n_tok] = tok[:, columns_of(flip(seq, c * group))].T
        for d in range(1, group):
            f_in[d, c].wait_recv()
            f_t[rows_c, d * n_tok : (d + 1) * n_tok] = f_buf[d, c].T

    loc_q.wait()
    loc_g.wait()
    for h in range(1, reach + 1):
        pl.when(seq >= h)(k_in[h - 1].wait_recv)

    scale = math.log2(math.e) / math.sqrt(HD)
    window = (reach + 1) * n_tok

    def head_of(k):
        return lax.rem(lax.div(sec, per_head) + 1 + k, KVH)

    r_in = {}

    def attend(k):
        head = head_of(k)
        key_head = keys[:, :, pl.ds(pl.multiple_of(head * HD, HD), HD)].reshape(window, HD)
        mask = jnp.concatenate([bias[...]] * PAIR, axis=1)
        acc = jnp.zeros((window, HD), F32)
        for r in range(0, GROUP, PAIR):
            def rows(ref):
                base = head * (GROUP * HD)
                parts = [
                    ref[:, pl.ds(pl.multiple_of(base + (r + i) * HD, HD), HD)] for i in range(PAIR)
                ]
                return jnp.concatenate(parts, axis=0)

            scores = lax.dot_general(
                key_head, rows(qry), (((1,), (1,)), ((), ())), preferred_element_type=F32
            ) * scale + mask
            top = jnp.max(scores, axis=0, keepdims=True)
            e = jnp.exp2(scores - top)
            p = e * (1.0 / jnp.sum(e, axis=0, keepdims=True))
            acc = acc + jnp.dot(p.astype(BF16), rows(grd), preferred_element_type=F32)
        own[k] = acc[0:n_tok]
        for h in range(1, reach + 1):
            ret_send[k, h - 1] = acc[h * n_tok : (h + 1) * n_tok].astype(BF16)
            copy = remote(
                ret_send.at[k, h - 1], ret_recv.at[k, h - 1],
                r_ssem.at[k, h - 1], r_rsem.at[k, h - 1], sec, seq - h,
            )
            pl.when(seq >= h)(copy.start)
            sends.append((seq >= h, copy))
            r_in[k, h] = copy

    v_in = {}

    def combine(k):
        value = own[k]
        for h in range(1, reach + 1):
            pl.when(seq + h < n_seq)(r_in[k, h].wait_recv)
            value = value + ret_recv[k, h - 1].astype(F32)
        vg[k, 0] = value.astype(BF16)
        for d in range(1, group):
            copy = remote(
                vg.at[k, 0], vg.at[k, d], v_ssem.at[k, d - 1], v_rsem.at[k, d - 1], sec, flip(seq, d)
            )
            launch(copy)
            v_in[k, d] = copy

    def finish(k):
        for d in range(1, group):
            v_in[k, d].wait_recv()
        result = jnp.dot(
            f_t[...], vg[k].reshape(group * n_tok, HD), preferred_element_type=F32
        )
        head = head_of(k)
        for i in range(per_head):
            piece = result[:, i * cs : (i + 1) * cs]
            slot = k * per_head + i
            to = head * per_head + i

            def give(slot=slot, to=to, piece=piece):
                rs_send[slot] = piece.astype(BF16)
                remote(
                    rs_send.at[slot], rs_recv.at[sec], s_ssem.at[slot], s_rsem.at[sec], to, seq
                ).start()

            copy = remote(
                rs_send.at[slot], rs_recv.at[sec], s_ssem.at[slot], s_rsem.at[sec], to, seq
            )
            if k < KVH - 1:
                give()
                sends.append((None, copy))
            else:
                if per_head > 1:
                    pl.when(to != sec)(give)
                    sends.append((to != sec, copy))

                @pl.when(to == sec)
                def _(piece=piece):
                    total_ref[...] = piece

    for step in range(KVH + 2):
        if step < KVH:
            attend(step)
        if 0 <= step - 1 < KVH:
            combine(step - 1)
        if 0 <= step - 2 < KVH:
            finish(step - 2)

    sources = [flip(sec, d) for d in range(1, n_sec)]
    for src in sources:
        remote(rs_recv.at[src], rs_recv.at[src], s_ssem.at[0], s_rsem.at[src], src, seq).wait_recv()
    theirs = pl.ds(f_cols, f_cols)
    away = total_ref[theirs, :]
    for src in sources:
        away = away + rs_recv[src, theirs, :].astype(F32)
    ex_send[...] = away.astype(BF16)
    swap = remote(ex_send, ex_recv, e_ssem.at[0], e_rsem.at[0], sec, other)
    launch(swap)
    mine = pl.ds(0, f_cols)
    final = total_ref[mine, :]
    for src in sources:
        final = final + rs_recv[src, mine, :].astype(F32)
    swap.wait_recv()
    out_ref[...] = final + ex_recv[...].astype(F32)

    for condition, copy in sends:
        if condition is None:
            copy.wait_send()
        else:
            pl.when(condition)(copy.wait_send)


def on_device(n_sec, n_seq, features, queries, out_grad, doc_ids, key_weight):
    tokens = features[0]
    n_tok, width = tokens.shape
    rows, kv_width = key_weight.shape
    reach = min(n_seq - 1, -(-(MOST - 1) // n_tok))
    half = rows // 2
    f_cols = width // n_seq
    group = n_seq // 2
    cs = kv_width // n_sec
    dma = lambda *shape: pltpu.SemaphoreType.DMA(shape)
    any_spec = pl.BlockSpec(memory_space=pltpu.HBM)
    vmem_spec = pl.BlockSpec(memory_space=pltpu.VMEM)
    return pl.pallas_call(
        functools.partial(kernel, n_sec, n_seq, reach),
        out_shape=jax.ShapeDtypeStruct((f_cols, cs), F32),
        in_specs=[any_spec, any_spec, any_spec, vmem_spec, any_spec],
        out_specs=vmem_spec,
        scratch_shapes=[
            pltpu.VMEM((n_tok, width), BF16),
            pltpu.VMEM((n_tok, HQ * HD), BF16),
            pltpu.VMEM((n_tok, HQ * HD), BF16),
            pltpu.VMEM((n_sec, 2, half, kv_width), BF16),
            pltpu.VMEM((group, 2, n_tok, f_cols), BF16),
            pltpu.VMEM((2 * f_cols, group * n_tok), BF16),
            pltpu.VMEM((reach + 1, n_tok, kv_width), BF16),
            pltpu.VMEM((reach + 1, 1, n_tok), jnp.int32),
            pltpu.VMEM(((reach + 1) * n_tok, n_tok), F32),
            pltpu.VMEM((KVH, reach, n_tok, HD), BF16),
            pltpu.VMEM((KVH, reach, n_tok, HD), BF16),
            pltpu.VMEM((KVH, n_tok, HD), F32),
            pltpu.VMEM((KVH, group, n_tok, HD), BF16),
            pltpu.VMEM((n_sec, 2 * f_cols, cs), BF16),
            pltpu.VMEM((n_sec, 2 * f_cols, cs), BF16),
            pltpu.VMEM((f_cols, cs), BF16),
            pltpu.VMEM((f_cols, cs), BF16),
            pltpu.VMEM((2 * f_cols, cs), F32),
            dma(4),
            dma(n_sec), dma(n_sec),
            dma(n_sec - 1), dma(n_sec - 1),
            dma(group - 1, 2), dma(group - 1, 2),
            dma(reach), dma(reach),
            dma(reach), dma(reach),
            dma(KVH, reach), dma(KVH, reach),
            dma(KVH, group - 1), dma(KVH, group - 1),
            dma(n_sec), dma(n_sec),
            dma(1), dma(1),
        ],
        compiler_params=pltpu.CompilerParams(
            collective_id=0, has_side_effects=True, vmem_limit_bytes=60 * 1024 * 1024
        ),
    )(tokens, queries[0], out_grad[0], doc_ids, key_weight.reshape(2, half, kv_width))


def solution(mesh):
    n_sec, n_seq = mesh.shape["section"], mesh.shape["seq"]
    return jax.shard_map(
        functools.partial(on_device, n_sec, n_seq),
        mesh=mesh,
        in_specs=(
            P("section", "seq", None),
            P("section", "seq", None),
            P("section", "seq", None),
            P("section", "seq"),
            P("section", None),
        ),
        out_specs=P("seq", "section"),
        check_vma=False,
    )
```

```python
import functools
import math

import jax
import jax.numpy as jnp
from jax import lax
from jax.experimental import pallas as pl
from jax.experimental.pallas import tpu as pltpu
from jax.sharding import PartitionSpec as P

HQ = 32
KVH = 4
HD = 128
MOST = 512
GROUP = HQ // KVH
PAIR = 2
MESH = pl.DeviceIdType.MESH
F32 = jnp.float32
BF16 = jnp.bfloat16


def flip(index, bits):
    bit = 1
    while bit <= bits:
        if bits & bit:
            index = index + bit * (1 - 2 * lax.rem(lax.div(index, bit), 2))
        bit *= 2
    return index


def kernel(
    n_sec, n_seq, reach,
    tok_hbm, qry_hbm, grd_hbm, doc_ref, kw_hbm,
    out_ref,
    tok, qry, grd, w_buf, f_buf, f_t, keys, docs, bias, ret_send, ret_recv, own, vg,
    rs_send, rs_recv, ex_send, ex_recv, total_ref,
    local_sem, w_ssem, w_rsem, x_ssem, x_rsem, f_ssem, f_rsem, d_ssem, d_rsem,
    k_ssem, k_rsem, r_ssem, r_rsem, v_ssem, v_rsem, s_ssem, s_rsem, e_ssem, e_rsem,
):
    sec, seq = lax.axis_index("section"), lax.axis_index("seq")
    core = lax.rem(seq, 2)
    n_tok = tok.shape[0]
    half = w_buf.shape[2]
    shard = 2 * half
    f_cols = f_buf.shape[3]
    group = n_seq // 2
    other = flip(seq, group)
    per_head = n_sec // KVH
    cs = rs_send.shape[2]

    def remote(src, dst, ssem, rsem, to_sec, to_seq):
        return pltpu.make_async_remote_copy(
            src_ref=src, dst_ref=dst, send_sem=ssem, recv_sem=rsem,
            device_id=(to_sec, to_seq), device_id_type=MESH,
        )

    loc_w = pltpu.make_async_copy(kw_hbm, w_buf.at[0], local_sem.at[0])
    loc_t = pltpu.make_async_copy(tok_hbm, tok, local_sem.at[1])
    loc_q = pltpu.make_async_copy(qry_hbm, qry, local_sem.at[2])
    loc_g = pltpu.make_async_copy(grd_hbm, grd, local_sem.at[3])

    barrier = pltpu.get_barrier_semaphore()
    for d in range(1, n_sec):
        pl.semaphore_signal(barrier, inc=1, device_id=(flip(sec, d), seq), device_id_type=MESH)
    for d in range(1, n_seq):
        pl.semaphore_signal(barrier, inc=1, device_id=(sec, flip(seq, d)), device_id_type=MESH)
    loc_w.start()
    loc_t.start()
    loc_q.start()
    loc_g.start()
    pl.semaphore_wait(barrier, n_sec + n_seq - 2)

    sends = []

    def launch(copy):
        copy.start()
        sends.append((None, copy))

    w_in = [None] + [
        remote(kw_hbm.at[core], w_buf.at[d, core], w_ssem.at[d - 1], w_rsem.at[d - 1], flip(sec, d), seq)
        for d in range(1, n_sec)
    ]
    relayed = n_sec == 4
    for d in range(1, n_sec - 1 if relayed else n_sec):
        launch(w_in[d])
    part = half // 2
    relay = [
        remote(
            w_buf.at[d, core, pl.ds(i * part, part)], w_buf.at[3, core, pl.ds(i * part, part)],
            w_ssem.at[2 + i], w_rsem.at[2 + i], flip(sec, 3 - d), seq,
        )
        for i, d in enumerate((1, 2))
    ] if relayed else []

    docs[0] = doc_ref[...]
    d_out = []
    for h in range(1, reach + 1):
        copy = remote(doc_ref, docs.at[h], d_ssem.at[h - 1], d_rsem.at[h - 1], sec, seq + h)
        d_out.append(copy)
        has_later = seq + h < n_seq
        pl.when(has_later)(copy.start)
        sends.append((has_later, copy))

    def columns_of(place):
        return pl.ds(pl.multiple_of(place * f_cols, f_cols), f_cols)

    f_in = {}
    for d in range(1, group):
        peer = flip(seq, d)
        for c in range(2):
            copy = remote(
                tok_hbm.at[:, columns_of(flip(peer, c * group))], f_buf.at[d, c],
                f_ssem.at[d - 1, c], f_rsem.at[d - 1, c], sec, peer,
            )
            launch(copy)
            f_in[d, c] = copy

    for h in range(1, reach + 1):
        @pl.when(seq < h)
        def _(h=h):
            docs[h] = jnp.full(docs.shape[1:], -1, jnp.int32)
            keys[h] = jnp.zeros(keys.shape[1:], BF16)

        @pl.when(seq + h >= n_seq)
        def _(h=h):
            for k in range(KVH):
                ret_recv[k, h - 1] = jnp.zeros(ret_recv.shape[2:], BF16)

    loc_t.wait()
    loc_w.wait()

    def project(d, which):
        row = pl.multiple_of(flip(sec, d) * shard + which * half, half)
        return jnp.dot(tok[:, pl.ds(row, half)], w_buf[d, which], preferred_element_type=F32)

    total = project(0, 0) + project(0, 1)

    own_row = docs[0]
    query_doc = own_row.astype(F32)
    key_at = lax.broadcasted_iota(jnp.int32, (n_tok, n_tok), 0)
    query_at = lax.broadcasted_iota(jnp.int32, (n_tok, n_tok), 1)
    for h in range(reach + 1):
        if h:
            pl.when(seq >= h)(d_out[h - 1].wait_recv)
        key_doc = jnp.broadcast_to(docs[h].astype(F32), (n_tok, n_tok)).T
        seen = key_doc == jnp.broadcast_to(query_doc, (n_tok, n_tok))
        if h == 0:
            seen = seen & (key_at <= query_at)
        bias[pl.ds(h * n_tok, n_tok), :] = jnp.where(seen, 0.0, -1e30)

    x_in = [None]
    for d in range(1, n_sec):
        if relayed and d == 3:
            for copy in relay:
                copy.wait_recv()
        else:
            w_in[d].wait_recv()
            if relayed:
                launch(relay[d - 1])
        copy = remote(
            w_buf.at[d, core], w_buf.at[d, core], x_ssem.at[d - 1], x_rsem.at[d - 1], sec, flip(seq, 1)
        )
        launch(copy)
        x_in.append(remote(
            w_buf.at[d, 1 - core], w_buf.at[d, 1 - core], x_ssem.at[d - 1], x_rsem.at[d - 1],
            sec, flip(seq, 1),
        ))
        total = total + project(d, core)
    for d in range(1, n_sec):
        x_in[d].wait_recv()
        total = total + project(d, 1 - core)
    keys[0] = total.astype(BF16)

    k_in = {}
    for h in range(2, reach + 1, 2):
        copy = remote(keys.at[0], keys.at[h], k_ssem.at[h - 1], k_rsem.at[h - 1], sec, seq + h)
        has_later = seq + h < n_seq
        pl.when(has_later)(copy.start)
        sends.append((has_later, copy))
        k_in[h] = copy

    def hand_on():
        for h in range(1, reach + 1, 2):
            pl.when(seq >= h + 1)(k_in[h + 1].wait_recv)
            from_slot = h - 1 + 2 * core
            copy = remote(
                keys.at[from_slot], keys.at[h], k_ssem.at[h - 1], k_rsem.at[h - 1], sec, flip(seq, 1)
            )
            pl.when(seq >= from_slot)(copy.start)
            sends.append((seq >= from_slot, copy))
            k_in[h] = copy

    for c in range(2):
        rows_c = pl.ds(c * f_cols, f_cols)
        f_t[rows_c, 0:n_tok] = tok[:, columns_of(flip(seq, c * group))].T
        for d in range(1, group):
            f_in[d, c].wait_recv()
            f_t[rows_c, d * n_tok : (d + 1) * n_tok] = f_buf[d, c].T
        if c == 0:
            hand_on()

    loc_q.wait()
    loc_g.wait()
    for h in range(1, reach + 1, 2):
        pl.when(seq >= h)(k_in[h].wait_recv)

    scale = math.log2(math.e) / math.sqrt(HD)
    window = (reach + 1) * n_tok

    def head_of(k):
        return lax.rem(lax.div(sec, per_head) + 1 + k, KVH)

    r_in = {}

    def attend(k):
        head = head_of(k)
        key_head = keys[:, :, pl.ds(pl.multiple_of(head * HD, HD), HD)].reshape(window, HD)
        mask = jnp.concatenate([bias[...]] * PAIR, axis=1)
        acc = jnp.zeros((window, HD), F32)
        for r in range(0, GROUP, PAIR):
            def rows(ref):
                base = head * (GROUP * HD)
                parts = [
                    ref[:, pl.ds(pl.multiple_of(base + (r + i) * HD, HD), HD)] for i in range(PAIR)
                ]
                return jnp.concatenate(parts, axis=0)

            scores = lax.dot_general(
                key_head, rows(qry), (((1,), (1,)), ((), ())), preferred_element_type=F32
            ) * scale + mask
            top = jnp.max(scores, axis=0, keepdims=True)
            e = jnp.exp2(scores - top)
            p = e * (1.0 / jnp.sum(e, axis=0, keepdims=True))
            acc = acc + jnp.dot(p.astype(BF16), rows(grd), preferred_element_type=F32)
        own[k] = acc[0:n_tok]
        for h in range(1, reach + 1):
            ret_send[k, h - 1] = acc[h * n_tok : (h + 1) * n_tok].astype(BF16)
            copy = remote(
                ret_send.at[k, h - 1], ret_recv.at[k, h - 1],
                r_ssem.at[k, h - 1], r_rsem.at[k, h - 1], sec, seq - h,
            )
            pl.when(seq >= h)(copy.start)
            sends.append((seq >= h, copy))
            r_in[k, h] = copy

    v_in = {}

    def combine(k):
        value = own[k]
        for h in range(1, reach + 1):
            pl.when(seq + h < n_seq)(r_in[k, h].wait_recv)
            value = value + ret_recv[k, h - 1].astype(F32)
        vg[k, 0] = value.astype(BF16)
        for d in range(1, group):
            copy = remote(
                vg.at[k, 0], vg.at[k, d], v_ssem.at[k, d - 1], v_rsem.at[k, d - 1], sec, flip(seq, d)
            )
            launch(copy)
            v_in[k, d] = copy

    def finish(k):
        for d in range(1, group):
            v_in[k, d].wait_recv()
        result = jnp.dot(
            f_t[...], vg[k].reshape(group * n_tok, HD), preferred_element_type=F32
        )
        head = head_of(k)
        for i in range(per_head):
            piece = result[:, i * cs : (i + 1) * cs]
            slot = k * per_head + i
            to = head * per_head + i

            def give(slot=slot, to=to, piece=piece):
                rs_send[slot] = piece.astype(BF16)
                remote(
                    rs_send.at[slot], rs_recv.at[sec], s_ssem.at[slot], s_rsem.at[sec], to, seq
                ).start()

            copy = remote(
                rs_send.at[slot], rs_recv.at[sec], s_ssem.at[slot], s_rsem.at[sec], to, seq
            )
            if k < KVH - 1:
                give()
                sends.append((None, copy))
            else:
                if per_head > 1:
                    pl.when(to != sec)(give)
                    sends.append((to != sec, copy))

                @pl.when(to == sec)
                def _(piece=piece):
                    total_ref[...] = piece

    for step in range(KVH + 2):
        if step < KVH:
            attend(step)
        if 0 <= step - 1 < KVH:
            combine(step - 1)
        if 0 <= step - 2 < KVH:
            finish(step - 2)

    sources = [flip(sec, d) for d in range(1, n_sec)]
    for src in sources:
        remote(rs_recv.at[src], rs_recv.at[src], s_ssem.at[0], s_rsem.at[src], src, seq).wait_recv()
    theirs = pl.ds(f_cols, f_cols)
    away = total_ref[theirs, :]
    for src in sources:
        away = away + rs_recv[src, theirs, :].astype(F32)
    ex_send[...] = away.astype(BF16)
    swap = remote(ex_send, ex_recv, e_ssem.at[0], e_rsem.at[0], sec, other)
    launch(swap)
    mine = pl.ds(0, f_cols)
    final = total_ref[mine, :]
    for src in sources:
        final = final + rs_recv[src, mine, :].astype(F32)
    swap.wait_recv()
    out_ref[...] = final + ex_recv[...].astype(F32)

    for condition, copy in sends:
        if condition is None:
            copy.wait_send()
        else:
            pl.when(condition)(copy.wait_send)


def on_device(n_sec, n_seq, features, queries, out_grad, doc_ids, key_weight):
    tokens = features[0]
    n_tok, width = tokens.shape
    rows, kv_width = key_weight.shape
    reach = min(n_seq - 1, -(-(MOST - 1) // n_tok))
    reach += reach % 2
    half = rows // 2
    f_cols = width // n_seq
    group = n_seq // 2
    cs = kv_width // n_sec
    dma = lambda *shape: pltpu.SemaphoreType.DMA(shape)
    any_spec = pl.BlockSpec(memory_space=pltpu.HBM)
    vmem_spec = pl.BlockSpec(memory_space=pltpu.VMEM)
    return pl.pallas_call(
        functools.partial(kernel, n_sec, n_seq, reach),
        out_shape=jax.ShapeDtypeStruct((f_cols, cs), F32),
        in_specs=[any_spec, any_spec, any_spec, vmem_spec, any_spec],
        out_specs=vmem_spec,
        scratch_shapes=[
            pltpu.VMEM((n_tok, width), BF16),
            pltpu.VMEM((n_tok, HQ * HD), BF16),
            pltpu.VMEM((n_tok, HQ * HD), BF16),
            pltpu.VMEM((n_sec, 2, half, kv_width), BF16),
            pltpu.VMEM((group, 2, n_tok, f_cols), BF16),
            pltpu.VMEM((2 * f_cols, group * n_tok), BF16),
            pltpu.VMEM((reach + 1, n_tok, kv_width), BF16),
            pltpu.VMEM((reach + 1, 1, n_tok), jnp.int32),
            pltpu.VMEM(((reach + 1) * n_tok, n_tok), F32),
            pltpu.VMEM((KVH, reach, n_tok, HD), BF16),
            pltpu.VMEM((KVH, reach, n_tok, HD), BF16),
            pltpu.VMEM((KVH, n_tok, HD), F32),
            pltpu.VMEM((KVH, group, n_tok, HD), BF16),
            pltpu.VMEM((n_sec, 2 * f_cols, cs), BF16),
            pltpu.VMEM((n_sec, 2 * f_cols, cs), BF16),
            pltpu.VMEM((f_cols, cs), BF16),
            pltpu.VMEM((f_cols, cs), BF16),
            pltpu.VMEM((2 * f_cols, cs), F32),
            dma(4),
            dma(n_sec), dma(n_sec),
            dma(n_sec - 1), dma(n_sec - 1),
            dma(group - 1, 2), dma(group - 1, 2),
            dma(reach), dma(reach),
            dma(reach), dma(reach),
            dma(KVH, reach), dma(KVH, reach),
            dma(KVH, group - 1), dma(KVH, group - 1),
            dma(n_sec), dma(n_sec),
            dma(1), dma(1),
        ],
        compiler_params=pltpu.CompilerParams(
            collective_id=0, has_side_effects=True, vmem_limit_bytes=60 * 1024 * 1024
        ),
    )(tokens, queries[0], out_grad[0], doc_ids, key_weight.reshape(2, half, kv_width))


def solution(mesh):
    n_sec, n_seq = mesh.shape["section"], mesh.shape["seq"]
    return jax.shard_map(
        functools.partial(on_device, n_sec, n_seq),
        mesh=mesh,
        in_specs=(
            P("section", "seq", None),
            P("section", "seq", None),
            P("section", "seq", None),
            P("section", "seq"),
            P("section", None),
        ),
        out_specs=P("seq", "section"),
        check_vma=False,
    )
```
